32 devices in a mesh: seq: 16 (over z, y, x), heads: 2 (over core).
Axes of the slice: x: 2, y: 2, z: 4, core: 2. Of those that a mesh axis runs over, the one named last changes fastest.
Arguments:
- hidden_in: bfloat16 [8192, 768], P('seq'), may hold values from -6 to 6
- memory: bfloat16 [8192, 768], P('seq'), may hold values from -6 to 6
- out_grad: bfloat16 [8192, 768], P('seq'), may hold values from -6 to 6
- norm_self: float32 [768], P('seq'), may hold values from 0.5 to 1.5
- self_q: float32 [768, 768], P('seq', 'heads'), may hold values from -0.4375 to 0.4375
- self_k: float32 [768, 768], P('seq', 'heads'), may hold values from -0.21875 to 0.21875
- self_v: float32 [768, 768], P('seq', 'heads'), may hold values from -0.21875 to 0.21875
- self_o: float32 [768, 768], P('heads', 'seq'), may hold values from -0.875 to 0.875
- norm_cross: float32 [768], P('seq'), may hold values from 0.5 to 1.5
- cross_q: float32 [768, 768], P('seq', 'heads'), may hold values from -0.4375 to 0.4375
- cross_k: float32 [768, 768], P('seq', 'heads'), may hold values from -0.21875 to 0.21875
- cross_v: float32 [768, 768], P('seq', 'heads'), may hold values from -0.21875 to 0.21875
- cross_o: float32 [768, 768], P('heads', 'seq'), may hold values from -0.875 to 0.875
- norm_ff: float32 [768], P('seq'), may hold values from 0.5 to 1.5
- ff_in: float32 [768, 3072], P('seq', 'heads'), may hold values from -0.21875 to 0.21875
- ff_out: float32 [3072, 768], P('heads', 'seq'), may hold values from -0.15625 to 0.15625
- bias_table: float32 [32, 12], P(None, 'heads'), may hold values from -4 to 4
- seg_ids: int32 [8192], replicated, may hold values from 0 to 32, as said below
- mem_seg: int32 [8192], replicated, may hold values from -1 to 32, as said below
- rel_bucket: int32 [1024], replicated, may hold values from 0 to 31, as said below
Outputs:
- mixed: bfloat16 [8192, 768], P('seq')
- grad_hidden: float32 [8192, 768], P('seq')
- grad_memory: float32 [8192, 768], P('seq')
- grad_norm_self: float32 [768], P('seq')
- grad_self_q: float32 [768, 768], P('seq', 'heads')
- grad_self_k: float32 [768, 768], P('seq', 'heads')
- grad_self_v: float32 [768, 768], P('seq', 'heads')
- grad_self_o: float32 [768, 768], P('heads', 'seq')
- grad_norm_cross: float32 [768], P('seq')
- grad_cross_q: float32 [768, 768], P('seq', 'heads')
- grad_cross_k: float32 [768, 768], P('seq', 'heads')
- grad_cross_v: float32 [768, 768], P('seq', 'heads')
- grad_cross_o: float32 [768, 768], P('heads', 'seq')
- grad_norm_ff: float32 [768], P('seq')
- grad_ff_in: float32 [768, 3072], P('seq', 'heads')
- grad_ff_out: float32 [3072, 768], P('heads', 'seq')
- grad_bias_table: float32 [32, 12], P(None, 'heads')
The draws below stay inside these ranges and needn't reach their ends.
Inputs may be any that keep to these rules, and one draw needn't show every extreme that they name: `seg_ids`: segment ids start at 0 and rise by 0 or 1 from one token to the next; they never rise at the first token of an aligned block of 512 tokens and rise 1 to 3 times inside each such block, so every segment lies in two neighbouring blocks. `mem_seg`: memory block k (the k-th aligned block of 512 tokens) holds a live prefix, then padding (-1); its live tokens carry, in order, the ids of the segments whose first token lies in target block k, each such segment one or more tokens. Some block is live throughout. rel_bucket[d] = d for d < 16; after that it never falls and rises by at most 1 from one distance to the next, reaching 31.
All inputs are finite; a program needn't handle non-finite values.
Results may differ from the reference program's by a relative error of at most 0.025.
The reference program's roundings to bfloat16 on the way count: a program that leaves them out, or rounds other values in their place, can miss the bound.
Values may be sent and summed in bfloat16 or wider, within the bound.
No kernel may reach another device: no remote copies, remote signals or barrier semaphores. Data moves between devices by JAX's collectives and lax.ppermute only.
A program may use at most 128 MiB of HBM per device.

```python
import math
import jax
import jax.numpy as jnp
from jax import lax

D = 768
H = 12
DH = 64
FF = 3072
NB = 32
TOK_DEV = 512
MEM_DEV = 512
TOKENS = 8192
MEMORY = 8192


def segment_cuts(key):
    blocks = TOKENS // TOK_DEV
    halves = jax.random.randint(jax.random.fold_in(key, 11), (blocks // 2,), 1, 4)
    counts = jnp.stack([halves, 4 - halves], axis=1).reshape(-1)
    block_keys = jax.random.split(jax.random.fold_in(key, 12), blocks)
    places = jax.vmap(lambda item: jax.random.permutation(item, TOK_DEV - 1))(block_keys) + 1
    ranks = jnp.arange(TOK_DEV - 1, dtype=jnp.int32)[None, :]
    chosen = (ranks < counts[:, None]).astype(jnp.int32)
    block_rows = jnp.arange(blocks, dtype=jnp.int32)[:, None]
    cuts = jnp.zeros((blocks, TOK_DEV), jnp.int32).at[block_rows, places].set(chosen)
    return jnp.cumsum(cuts.reshape(-1)).astype(jnp.int32)


def draw_seg_ids(key, part):
    segments = segment_cuts(key)
    return segments


def draw_mem_seg(key, part):
    segments = segment_cuts(key)
    key = jax.random.fold_in(key, 2)
    blocks = TOKENS // TOK_DEV
    grid = segments.reshape(blocks, TOK_DEV)
    first_ids = grid[:, 0] + (jnp.arange(blocks, dtype=jnp.int32) > 0).astype(jnp.int32)
    count_ids = grid[:, -1] - first_ids + 1
    live = jax.random.randint(jax.random.fold_in(key, 1), (blocks,), MEM_DEV // 4, MEM_DEV + 1)
    full_block = jax.random.randint(jax.random.fold_in(key, 2), (), 0, blocks)
    live = live.at[full_block].set(MEM_DEV)
    slots = jnp.arange(MEM_DEV, dtype=jnp.int32)[None, :]
    owners = first_ids[:, None] + slots * count_ids[:, None] // live[:, None]
    return jnp.where(slots < live[:, None], owners, -1).reshape(-1).astype(jnp.int32)


def draw_rel_bucket(key, part):
    key = jax.random.fold_in(key, 3)
    span = 2 * TOK_DEV - NB // 2
    places = jax.random.permutation(key, span - 1) + 1
    steps = jnp.zeros((span,), jnp.int32).at[places[:NB // 2 - 1]].set(1)
    tail = NB // 2 + jnp.cumsum(steps)
    return jnp.concatenate([jnp.arange(NB // 2, dtype=jnp.int32), tail.astype(jnp.int32)])


def steps_of(stream_key, shape, pieces, low, high):
    gain = 1.0
    for position, parts in pieces:
        draws = jax.random.uniform(jax.random.fold_in(jax.random.fold_in(stream_key, 6), position), (parts,), jnp.float32, low / len(pieces), high / len(pieces))
        gain = gain * jnp.repeat(jnp.exp(draws), shape[position] // parts).reshape((-1,) + (1,) * (len(shape) - 1 - position))
    return gain


def normal_values(rng, extent, scale, reach, pieces=(), kind=jnp.bfloat16):
    level = steps_of(rng, extent, pieces, -0.22, 0.18) if pieces else 1.0
    values = jax.random.normal(rng, extent, jnp.float32) * scale * level
    return jnp.minimum(jnp.maximum(values, -reach), reach).astype(kind)


def setup_inputs(seed: int = 0) -> dict:
    arg_keys = jax.random.split(jax.random.key(seed), 21)
    hidden_in = normal_values(arg_keys[0], (TOKENS, D), 1.0, 6.0, ((0, 16),))
    memory = normal_values(arg_keys[1], (MEMORY, D), 1.0, 6.0, ((0, 16),))
    out_grad = normal_values(arg_keys[2], (TOKENS, D), 1.0, 6.0, ((0, 16),))
    norm_self = jnp.clip(1.0 + 0.1 * jax.random.normal(arg_keys[3], (D,), jnp.float32), 0.5, 1.5)
    self_q = normal_values(arg_keys[4], (D, H * DH), (D // 4) ** -0.5, 0.4375, ((0, 16), (1, 2)), jnp.float32)
    self_k = normal_values(arg_keys[5], (D, H * DH), D ** -0.5, 0.21875, ((0, 16), (1, 2)), jnp.float32)
    self_v = normal_values(arg_keys[6], (D, H * DH), D ** -0.5, 0.21875, ((0, 16), (1, 2)), jnp.float32)
    self_o = normal_values(arg_keys[7], (H * DH, D), (H * DH // 16) ** -0.5, 0.875, ((0, 2), (1, 16)), jnp.float32)
    norm_cross = jnp.clip(1.0 + 0.1 * jax.random.normal(arg_keys[8], (D,), jnp.float32), 0.5, 1.5)
    cross_q = normal_values(arg_keys[9], (D, H * DH), (D // 4) ** -0.5, 0.4375, ((0, 16), (1, 2)), jnp.float32)
    cross_k = normal_values(arg_keys[10], (D, H * DH), D ** -0.5, 0.21875, ((0, 16), (1, 2)), jnp.float32)
    cross_v = normal_values(arg_keys[11], (D, H * DH), D ** -0.5, 0.21875, ((0, 16), (1, 2)), jnp.float32)
    cross_o = normal_values(arg_keys[12], (H * DH, D), (H * DH // 16) ** -0.5, 0.875, ((0, 2), (1, 16)), jnp.float32)
    norm_ff = jnp.clip(1.0 + 0.1 * jax.random.normal(arg_keys[13], (D,), jnp.float32), 0.5, 1.5)
    ff_in = normal_values(arg_keys[14], (D, FF), D ** -0.5, 0.21875, ((0, 16), (1, 2)), jnp.float32)
    ff_out = normal_values(arg_keys[15], (FF, D), (FF // 2) ** -0.5, 0.15625, ((0, 2), (1, 16)), jnp.float32)
    bias_table = normal_values(arg_keys[16], (NB, H), 1.0, 4.0, ((1, 2),), jnp.float32)
    seg_ids = draw_seg_ids(jax.random.fold_in(arg_keys[20], 71), 0)
    mem_seg = draw_mem_seg(jax.random.fold_in(arg_keys[20], 71), 0)
    rel_bucket = draw_rel_bucket(jax.random.fold_in(arg_keys[20], 71), 0)
    return {"hidden_in": hidden_in, "memory": memory, "out_grad": out_grad, "norm_self": norm_self, "self_q": self_q, "self_k": self_k, "self_v": self_v, "self_o": self_o, "norm_cross": norm_cross, "cross_q": cross_q, "cross_k": cross_k, "cross_v": cross_v, "cross_o": cross_o, "norm_ff": norm_ff, "ff_in": ff_in, "ff_out": ff_out, "bias_table": bias_table, "seg_ids": seg_ids, "mem_seg": mem_seg, "rel_bucket": rel_bucket}


EPSILON = 1e-06
MASKED = -1000000000.0

@jax.custom_vjp
def low(v):
    return lax.optimization_barrier(v.astype(jnp.bfloat16)).astype(jnp.float32)

@jax.custom_vjp
def low_back(v):
    return v

def low_keep(v):
    return (low(v), None)

def low_pass(kept, grad):
    return (grad,)

def back_keep(v):
    return (v, None)

def back_low(kept, grad):
    return (low(grad),)
low.defvjp(low_keep, low_pass)
low_back.defvjp(back_keep, back_low)

def rms_scale(values):
    return values * lax.rsqrt(lax.optimization_barrier(jnp.mean(values * values, axis=-1, keepdims=True)) + EPSILON)

def exact_dot(left, right):
    return jnp.dot(left, right, precision=lax.Precision.HIGHEST, preferred_element_type=jnp.float32)

def attend(queries, keys, values, allowed, rel_bias, factor):
    scores = jnp.einsum('ihd,jhd->hij', queries, keys, precision=lax.Precision.HIGHEST) * factor + rel_bias
    scores = low_back(scores)
    scores = jnp.where(allowed[None], scores, MASKED)
    peak = lax.optimization_barrier(jnp.max(scores, axis=-1, keepdims=True))
    raised = jnp.exp(scores - peak)
    weights = raised / lax.optimization_barrier(jnp.sum(raised, axis=-1, keepdims=True))
    return jnp.einsum('hij,jhd->ihd', low(weights), values, precision=lax.Precision.HIGHEST)

def reference(hidden_in, memory, out_grad, norm_self, self_q, self_k, self_v, self_o, norm_cross, cross_q, cross_k, cross_v, cross_o, norm_ff, ff_in, ff_out, bias_table, seg_ids, mem_seg, rel_bucket):

    def forward(stream_in, memory_in, norm_self, self_q, self_k, self_v, self_o, norm_cross, cross_q, cross_k, cross_v, cross_o, norm_ff, ff_in, ff_out, bias_table):
        tokens = stream_in.shape[0]
        mem_tokens = memory_in.shape[0]
        heads = bias_table.shape[1]
        head_size = self_q.shape[1] // heads
        factor = head_size ** (-0.5)
        block = math.gcd(tokens, 256)
        positions = jnp.arange(tokens, dtype=jnp.int32)
        starts = jnp.arange(0, tokens, block, dtype=jnp.int32)

        def project(normed, weight):
            return low_back(low(exact_dot(normed, low(weight))))
        normed_one = low(rms_scale(stream_in) * low(norm_self))
        query_one = project(normed_one, self_q).reshape(tokens, heads, head_size)
        key_one = project(normed_one, self_k).reshape(tokens, heads, head_size)
        value_one = project(normed_one, self_v).reshape(tokens, heads, head_size)
        mem_key = project(memory_in, cross_k).reshape(mem_tokens, heads, head_size)
        mem_value = project(memory_in, cross_v).reshape(mem_tokens, heads, head_size)

        def self_block(start):
            query_part = lax.dynamic_slice_in_dim(query_one, start, block, 0)
            seg_part = lax.dynamic_slice_in_dim(seg_ids, start, block, 0)
            distance = (start + jnp.arange(block, dtype=jnp.int32))[:, None] - positions[None, :]
            allowed = (seg_part[:, None] == seg_ids[None, :]) & (distance >= 0)
            bucket = rel_bucket[jnp.clip(distance, 0, rel_bucket.shape[0] - 1)]
            rel_bias = jnp.moveaxis(bias_table[bucket], 2, 0)
            return attend(query_part, key_one, value_one, allowed, rel_bias, factor)
        attended = lax.map(jax.checkpoint(self_block), starts).reshape(tokens, heads * head_size)
        attend_one = low_back(low(attended))
        stream_one = stream_in + low_back(exact_dot(attend_one, low(self_o)))
        normed_two = low(rms_scale(stream_one) * low(norm_cross))
        query_two = project(normed_two, cross_q).reshape(tokens, heads, head_size)

        def cross_block(start):
            query_part = lax.dynamic_slice_in_dim(query_two, start, block, 0)
            seg_part = lax.dynamic_slice_in_dim(seg_ids, start, block, 0)
            allowed = seg_part[:, None] == mem_seg[None, :]
            return attend(query_part, mem_key, mem_value, allowed, 0.0, factor)
        attended_two = lax.map(jax.checkpoint(cross_block), starts).reshape(tokens, heads * head_size)
        attend_two = low_back(low(attended_two))
        stream_two = stream_one + low_back(exact_dot(attend_two, low(cross_o)))
        normed_three = low(rms_scale(stream_two) * low(norm_ff))
        hidden_pre = low_back(exact_dot(normed_three, low(ff_in)))
        active = low(jax.nn.gelu(hidden_pre))
        return stream_two + low_back(exact_dot(active, low(ff_out)))
    masters = tuple((item.astype(jnp.float32) for item in (norm_self, self_q, self_k, self_v, self_o, norm_cross, cross_q, cross_k, cross_v, cross_o, norm_ff, ff_in, ff_out, bias_table)))
    result, pull = jax.vjp(forward, hidden_in.astype(jnp.float32), memory.astype(jnp.float32), *masters)
    grads = pull(out_grad.astype(jnp.float32))
    return (result.astype(jnp.bfloat16), grads[0], grads[1], grads[2], grads[3], grads[4], grads[5], grads[6], grads[7], grads[8], grads[9], grads[10], grads[11], grads[12], grads[13], grads[14], grads[15])
```

```python
import jax
import jax.numpy as jnp
from jax import lax
from jax.sharding import PartitionSpec as P

EPSILON = 1e-06
MASKED = -1000000000.0


def shifted(value, axis, steps):
    count = lax.axis_size(axis)
    leading, last = (max(0, -steps), min(count, count - steps))
    return lax.ppermute(value, axis, [(source, source + steps) for source in range(leading, last)])


def rms_scale(values):
    return values * lax.rsqrt(jnp.mean(values * values, axis=-1, keepdims=True) + EPSILON)


def norm_apply(values, gain):
    return rms_scale(values) * gain


def matmul(spec, left, right):
    return jnp.einsum(spec, left, right, preferred_element_type=jnp.float32)


def split_heads(values, local_heads):
    return values.reshape(values.shape[0], local_heads, values.shape[1] // local_heads)


def merge_heads(values):
    return values.reshape(values.shape[0], values.shape[1] * values.shape[2])


def head_sum(values):
    other = lax.ppermute(values, "heads", [(0, 1), (1, 0)])
    return jax.tree.map(jnp.add, values, other)


def masked_scores(queries, keys, allowed, rel_bias, factor):
    scores = matmul("ihd,jhd->hij", queries, keys) * factor + rel_bias
    return jnp.where(allowed[None], scores, MASKED)


def attend_forward(queries, keys, values, allowed, rel_bias, factor):
    scores = masked_scores(queries, keys, allowed, rel_bias, factor)
    peak = jnp.max(scores, axis=-1, keepdims=True)
    raised = jnp.exp(scores - peak)
    totals = jnp.sum(raised, axis=-1, keepdims=True)
    weights = (raised / totals).astype(jnp.bfloat16)
    return (matmul("hij,jhd->ihd", weights, values), peak + jnp.log(totals))


def attend_backward(queries, keys, values, allowed, rel_bias, logsum, grad_out, factor):
    weights = jnp.exp(masked_scores(queries, keys, allowed, rel_bias, factor) - logsum)
    grad_weights = matmul("ihd,jhd->hij", grad_out, values)
    inner = jnp.sum(weights * grad_weights, axis=-1, keepdims=True)
    grad_scores = (weights * (grad_weights - inner)).astype(jnp.bfloat16)
    grad_queries = matmul("hij,jhd->ihd", grad_scores, keys) * factor
    grad_keys = matmul("hij,ihd->jhd", grad_scores, queries) * factor
    grad_values = matmul("hij,ihd->jhd", weights.astype(jnp.bfloat16), grad_out)
    return (grad_queries, grad_keys, grad_values, grad_scores)


def axis_bits(axis):
    return lax.axis_size(axis).bit_length() - 1


def bit_orders(bits):
    high = list(range(bits - 1, 1, -1))
    low = list(range(min(bits, 2)))
    return high + low[::-1], high + low


def partner_swap(value, axis, bit):
    count = lax.axis_size(axis)
    return lax.ppermute(value, axis, [(i, i ^ (1 << bit)) for i in range(count)])


def my_bit(axis, bit):
    return (lax.axis_index(axis) >> bit) & 1


def gather_rows(shard, axis):
    bits = axis_bits(axis)
    cut = shard.shape[1] // 256 * 128
    halves = []
    for order, part in zip(bit_orders(bits), (shard[:, :cut], shard[:, cut:])):
        done = []
        value = part
        for bit in order:
            other = partner_swap(value, axis, bit)
            place = sum(1 for b in done if b > bit)
            mine = my_bit(axis, bit) == 0
            value = jnp.stack(
                [jnp.where(mine, value, other), jnp.where(mine, other, value)], axis=place
            )
            done.append(bit)
        halves.append(value.reshape(-1, part.shape[1]))
    return jnp.concatenate(halves, axis=1)


def scatter_rows(full, axis):
    bits = axis_bits(axis)
    cut = full.shape[1] // 256 * 128
    halves = []
    for order, part in zip(bit_orders(bits), (full[:, :cut], full[:, cut:])):
        value = part.reshape((2,) * bits + (-1, part.shape[1]))
        left = list(range(bits - 1, -1, -1))
        for bit in order[::-1]:
            place = left.index(bit)
            mine = my_bit(axis, bit)
            keep = lax.dynamic_index_in_dim(value, mine, place, keepdims=False)
            send = lax.dynamic_index_in_dim(value, 1 - mine, place, keepdims=False)
            got = partner_swap(send.astype(jnp.bfloat16), axis, bit)
            value = keep + got.astype(jnp.float32)
            left.remove(bit)
        halves.append(value)
    return jnp.concatenate(halves, axis=1)


def sum_all(value, axis):
    for bit in range(axis_bits(axis)):
        value = value + partner_swap(value, axis, bit)
    return value


def per_device(
    hidden_in,
    memory,
    out_grad,
    norm_self,
    self_q,
    self_k,
    self_v,
    self_o,
    norm_cross,
    cross_q,
    cross_k,
    cross_v,
    cross_o,
    norm_ff,
    ff_in,
    ff_out,
    bias_table,
    seg_ids,
    mem_seg,
    rel_bucket,
):
    low_type = jnp.bfloat16
    part = self_q.shape[1]
    wide = ff_in.shape[1]
    gains = jnp.pad(jnp.stack([norm_self, norm_cross, norm_ff], axis=1), ((0, 0), (0, 125)))
    first = gather_rows(
        jnp.concatenate([gains, self_q, self_k, self_v], axis=1).astype(low_type), "seq"
    )
    second = gather_rows(
        jnp.concatenate([cross_k, cross_v, self_o.T, cross_q, cross_o.T], axis=1).astype(low_type),
        "seq",
    )
    third = gather_rows(jnp.concatenate([ff_in, ff_out.T], axis=1).astype(low_type), "seq")
    gain_self, gain_cross, gain_ff = first[:, 0], first[:, 1], first[:, 2]
    query_self, key_self, value_self = (first[:, 128 + i * part : 128 + (i + 1) * part] for i in range(3))
    key_cross, value_cross, out_self, query_cross, out_cross = (
        second[:, i * part : (i + 1) * part] for i in range(5)
    )
    ff_up, ff_down = third[:, :wide], third[:, wide:]
    row_count = hidden_in.shape[0]
    mem_count = memory.shape[0]
    local_heads = bias_table.shape[1]
    local_width = self_q.shape[1]
    bucket_count = bias_table.shape[0]
    factor = (local_width // local_heads) ** (-0.5)
    position = lax.axis_index("seq")
    earlier = position > 0
    seg_own = lax.dynamic_slice_in_dim(seg_ids, position * row_count, row_count)
    seg_before = lax.dynamic_slice_in_dim(
        seg_ids, jnp.maximum(position - 1, 0) * row_count, row_count
    )
    mem_own = lax.dynamic_slice_in_dim(mem_seg, position * mem_count, mem_count)
    mem_before = lax.dynamic_slice_in_dim(
        mem_seg, jnp.maximum(position - 1, 0) * mem_count, mem_count
    )
    seg_keys = jnp.concatenate([seg_before, seg_own])
    mem_keys = jnp.concatenate([mem_before, mem_own])
    query_index = jnp.arange(row_count, dtype=jnp.int32)[:, None]
    key_index = jnp.arange(2 * row_count, dtype=jnp.int32)[None, :]
    distance = query_index + row_count - key_index
    self_allowed = (
        (seg_own[:, None] == seg_keys[None, :])
        & (distance >= 0)
        & (earlier | (key_index >= row_count))
    )
    mem_index = jnp.arange(2 * mem_count, dtype=jnp.int32)[None, :]
    cross_allowed = (seg_own[:, None] == mem_keys[None, :]) & (earlier | (mem_index >= mem_count))
    bucket_edges = jnp.sum(
        (rel_bucket[:, None] < jnp.arange(bucket_count + 1, dtype=jnp.int32)[None, :]).astype(
            jnp.int32
        ),
        axis=0,
    )
    pair_table = (distance[:, :, None] >= bucket_edges[None, None, :-1]) & (
        distance[:, :, None] < bucket_edges[None, None, 1:]
    )
    rel_bias = jnp.einsum(
        "ijb,bh->hij", pair_table.astype(jnp.float32), bias_table, precision=lax.Precision.HIGHEST
    )
    stream_in = hidden_in.astype(jnp.float32)
    normed_one = norm_apply(stream_in, gain_self.astype(jnp.float32)).astype(low_type)
    query_one = matmul("td,dw->tw", normed_one, query_self).astype(low_type)
    key_one = matmul("td,dw->tw", normed_one, key_self).astype(low_type)
    value_one = matmul("td,dw->tw", normed_one, value_self).astype(low_type)
    mem_key = matmul("md,dw->mw", memory, key_cross).astype(low_type)
    mem_value = matmul("md,dw->mw", memory, value_cross).astype(low_type)
    before = shifted((key_one, value_one, mem_key, mem_value), "seq", 1)
    keys_self = split_heads(jnp.concatenate([before[0], key_one]), local_heads)
    values_self = split_heads(jnp.concatenate([before[1], value_one]), local_heads)
    keys_mem = split_heads(jnp.concatenate([before[2], mem_key]), local_heads)
    values_mem = split_heads(jnp.concatenate([before[3], mem_value]), local_heads)
    queries_one = split_heads(query_one, local_heads)
    attended_one, logsum_one = attend_forward(
        queries_one, keys_self, values_self, self_allowed, rel_bias, factor
    )
    attend_one = merge_heads(attended_one).astype(low_type)
    stream_one = stream_in + head_sum(matmul("tw,dw->td", attend_one, out_self))
    normed_two = norm_apply(stream_one, gain_cross.astype(jnp.float32)).astype(low_type)
    query_two = matmul("td,dw->tw", normed_two, query_cross).astype(low_type)
    queries_two = split_heads(query_two, local_heads)
    attended_two, logsum_two = attend_forward(
        queries_two, keys_mem, values_mem, cross_allowed, 0.0, factor
    )
    attend_two = merge_heads(attended_two).astype(low_type)
    stream_two = stream_one + head_sum(matmul("tw,dw->td", attend_two, out_cross))
    normed_three = norm_apply(stream_two, gain_ff.astype(jnp.float32)).astype(low_type)
    hidden_pre = matmul("td,df->tf", normed_three, ff_up)
    active = jax.nn.gelu(hidden_pre).astype(low_type)
    stream_out = stream_two + head_sum(matmul("tf,df->td", active, ff_down))
    mixed = stream_out.astype(low_type)
    grad_out = out_grad.astype(jnp.float32)
    grad_down = matmul("td,tf->df", out_grad, active)
    grad_active = matmul("td,df->tf", out_grad, ff_down)
    gelu_value, gelu_pull = jax.vjp(jax.nn.gelu, hidden_pre)
    grad_pre = gelu_pull(grad_active)[0].astype(low_type)
    grad_up = matmul("td,tf->df", normed_three, grad_pre)
    grad_normed_three = head_sum(matmul("tf,df->td", grad_pre, ff_up))
    norm_value, norm_pull = jax.vjp(norm_apply, stream_two, gain_ff.astype(jnp.float32))
    grad_stream_three, grad_gain_ff = norm_pull(grad_normed_three)
    grad_two = grad_out + grad_stream_three
    ff_summed = scatter_rows(jnp.concatenate([grad_up, grad_down], axis=1), "seq")
    low_two = grad_two.astype(low_type)
    grad_out_cross = matmul("td,tw->dw", low_two, attend_two)
    grad_attend_two = split_heads(
        matmul("td,dw->tw", low_two, out_cross).astype(low_type), local_heads
    )
    grad_queries_two, grad_mem_keys, grad_mem_values, unused_scores = attend_backward(
        queries_two, keys_mem, values_mem, cross_allowed, 0.0, logsum_two, grad_attend_two, factor
    )
    grad_query_two = merge_heads(grad_queries_two).astype(low_type)
    grad_query_cross = matmul("td,tw->dw", normed_two, grad_query_two)
    grad_normed_two = head_sum(matmul("tw,dw->td", grad_query_two, query_cross))
    norm_value, norm_pull = jax.vjp(norm_apply, stream_one, gain_cross.astype(jnp.float32))
    grad_stream_two, grad_gain_cross = norm_pull(grad_normed_two)
    grad_one = grad_two + grad_stream_two
    cross_summed = scatter_rows(jnp.concatenate([grad_query_cross, grad_out_cross], axis=1), "seq")
    low_one = grad_one.astype(low_type)
    grad_out_self = matmul("td,tw->dw", low_one, attend_one)
    grad_attend_one = split_heads(
        matmul("td,dw->tw", low_one, out_self).astype(low_type), local_heads
    )
    grad_queries_one, grad_keys_self, grad_values_self, grad_scores = attend_backward(
        queries_one,
        keys_self,
        values_self,
        self_allowed,
        rel_bias,
        logsum_one,
        grad_attend_one,
        factor,
    )
    grad_table_part = matmul("hij,ijb->bh", grad_scores, pair_table.astype(low_type))
    flat_keys = merge_heads(grad_keys_self)
    flat_values = merge_heads(grad_values_self)
    flat_mem_keys = merge_heads(grad_mem_keys)
    flat_mem_values = merge_heads(grad_mem_values)
    later = (
        shifted(flat_keys[:row_count].astype(jnp.bfloat16), "seq", -1).astype(jnp.float32),
        shifted(flat_values[:row_count].astype(jnp.bfloat16), "seq", -1).astype(jnp.float32),
        shifted(flat_mem_keys[:mem_count].astype(jnp.bfloat16), "seq", -1).astype(jnp.float32),
        shifted(flat_mem_values[:mem_count].astype(jnp.bfloat16), "seq", -1).astype(jnp.float32),
    )
    grad_key_one = (flat_keys[row_count:] + later[0]).astype(low_type)
    grad_value_one = (flat_values[row_count:] + later[1]).astype(low_type)
    grad_mem_key = (flat_mem_keys[mem_count:] + later[2]).astype(low_type)
    grad_mem_value = (flat_mem_values[mem_count:] + later[3]).astype(low_type)
    grad_query_one = merge_heads(grad_queries_one).astype(low_type)
    grad_query_self = matmul("td,tw->dw", normed_one, grad_query_one)
    grad_key_self = matmul("td,tw->dw", normed_one, grad_key_one)
    grad_value_self = matmul("td,tw->dw", normed_one, grad_value_one)
    grad_key_cross = matmul("md,mw->dw", memory, grad_mem_key)
    grad_value_cross = matmul("md,mw->dw", memory, grad_mem_value)
    normed_part = (
        matmul("tw,dw->td", grad_query_one, query_self)
        + matmul("tw,dw->td", grad_key_one, key_self)
        + matmul("tw,dw->td", grad_value_one, value_self)
    )
    memory_part = matmul("mw,dw->md", grad_mem_key, key_cross) + matmul(
        "mw,dw->md", grad_mem_value, value_cross
    )
    grad_normed_one, grad_memory = head_sum((normed_part, memory_part))
    norm_value, norm_pull = jax.vjp(norm_apply, stream_in, gain_self.astype(jnp.float32))
    grad_stream_one, grad_gain_self = norm_pull(grad_normed_one)
    grad_hidden = grad_one + grad_stream_one
    gain_grads = jnp.pad(jnp.stack([grad_gain_self, grad_gain_cross, grad_gain_ff], axis=1), ((0, 0), (0, 125)))
    rest_summed = scatter_rows(
        jnp.concatenate(
            [gain_grads, grad_query_self, grad_key_self, grad_value_self, grad_out_self, grad_key_cross, grad_value_cross],
            axis=1,
        ),
        "seq",
    )
    rest = [rest_summed[:, 128 + i * part : 128 + (i + 1) * part] for i in range(6)]
    grad_table = sum_all(grad_table_part, "seq")
    return (
        mixed,
        grad_hidden,
        grad_memory,
        rest_summed[:, 0],
        rest[0],
        rest[1],
        rest[2],
        rest[3].T,
        rest_summed[:, 1],
        cross_summed[:, :part],
        rest[4],
        rest[5],
        cross_summed[:, part:].T,
        rest_summed[:, 2],
        ff_summed[:, :wide],
        ff_summed[:, wide:].T,
        grad_table,
    )


def solution(mesh):
    in_specs = (
        P("seq", None),
        P("seq", None),
        P("seq", None),
        P("seq"),
        P("seq", "heads"),
        P("seq", "heads"),
        P("seq", "heads"),
        P("heads", "seq"),
        P("seq"),
        P("seq", "heads"),
        P("seq", "heads"),
        P("seq", "heads"),
        P("heads", "seq"),
        P("seq"),
        P("seq", "heads"),
        P("heads", "seq"),
        P(None, "heads"),
        P(),
        P(),
        P(),
    )
    out_specs = (
        P("seq", None),
        P("seq", None),
        P("seq", None),
        P("seq"),
        P("seq", "heads"),
        P("seq", "heads"),
        P("seq", "heads"),
        P("heads", "seq"),
        P("seq"),
        P("seq", "heads"),
        P("seq", "heads"),
        P("seq", "heads"),
        P("heads", "seq"),
        P("seq"),
        P("seq", "heads"),
        P("heads", "seq"),
        P(None, "heads"),
    )
    return jax.shard_map(
        per_device, mesh=mesh, in_specs=in_specs, out_specs=out_specs, check_vma=False
    )
```

```python
import functools

import jax
import jax.numpy as jnp
from jax import lax
from jax.experimental import pallas as pl
from jax.experimental.pallas import tpu as pltpu
from jax.sharding import Mesh, PartitionSpec as P

EPSILON = 1e-06
MASKED = -1000000000.0
LANES = 128
TILE = 256
VMEM_LIMIT = 56 * 2**20
GELU_ROOT = 0.7978845608028654
GELU_CUBE = 0.044715


def dot_nt(left, right):
    return lax.dot_general(left, right, (((1,), (1,)), ((), ())), preferred_element_type=jnp.float32)


def dot_nn(left, right):
    return jnp.dot(left, right, preferred_element_type=jnp.float32)


def dot_tn(left, right):
    return lax.dot_general(left, right, (((0,), (0,)), ((), ())), preferred_element_type=jnp.float32)


def low(value):
    return value.astype(jnp.bfloat16)


def full_block(shape):
    return pl.BlockSpec(shape, lambda i: (0,) * len(shape))


def params(flops, nbytes):
    return dict(
        compiler_params=pltpu.CompilerParams(vmem_limit_bytes=VMEM_LIMIT),
        cost_estimate=pl.CostEstimate(flops=flops, bytes_accessed=nbytes, transcendentals=0),
    )


def bias_kernel(rel_ref, table_ref, out_ref):
    heads, span = out_ref.shape[0], rel_ref.shape[1]
    count = span // LANES
    buckets = table_ref.shape[1]
    rel = rel_ref[...]
    by_distance = jnp.zeros((table_ref.shape[0], span), jnp.float32)
    for bucket in range(buckets):
        by_distance = jnp.where(rel == bucket, table_ref[:, bucket : bucket + 1], by_distance)
    rows = lax.broadcasted_iota(jnp.int32, (LANES, LANES), 0)
    cols = lax.broadcasted_iota(jnp.int32, (LANES, LANES), 1)
    for head in range(heads):
        line = by_distance[head : head + 1]
        for block in range(count):
            before = (block - 1) % count
            window = jnp.concatenate(
                [
                    line[:, block * LANES : (block + 1) * LANES],
                    line[:, before * LANES : (before + 1) * LANES],
                ],
                axis=1,
            )
            window = jnp.broadcast_to(window, (LANES, 2 * LANES))
            tile = pltpu.roll(window, 0, 1, stride=1, stride_axis=0)[:, :LANES]
            if block == 0:
                tile = jnp.where(cols >= rows, tile, MASKED)
            start = (count - 1 - block) * LANES
            out_ref[head, start : start + LANES, :] = tile
        out_ref[head, span : span + LANES, :] = jnp.full((LANES, LANES), MASKED, jnp.float32)


def bias_tiles(rel_row, bias_table):
    span = rel_row.shape[1]
    buckets, heads = bias_table.shape
    table = jnp.pad(bias_table.T, ((0, 8 - heads), (0, 0)))
    return pl.pallas_call(
        bias_kernel,
        out_shape=jax.ShapeDtypeStruct((heads, span + LANES, LANES), jnp.float32),
        name="bias_tiles",
        **params(10**9, 4 * 10**6),
    )(rel_row, table)


def head_lanes(values, head, size):
    lane = lax.broadcasted_iota(jnp.int32, values.shape, 1)
    return jnp.where((lane >= head * size) & (lane < (head + 1) * size), values, jnp.zeros_like(values))


def key_rows(causal, tile, rows, keys):
    return keys - rows + (tile + 1) * TILE if causal else keys


def bias_at(bias_ref, head, tile, rows, need):
    parts = []
    for sub in range(TILE // LANES):
        start = (rows // LANES - 1 - (tile * (TILE // LANES) + sub)) * LANES
        parts.append(bias_ref[head, start : start + need, :])
    return jnp.concatenate(parts, axis=1)


def attend(queries, k, v, seg_ref, own_ref, bias_ref, att_ref, p_ref, size):
    rows, keys = queries.shape[0], k.shape[0]
    causal = bias_ref is not None
    queries = queries * jnp.asarray(size**-0.5, queries.dtype)
    flipped = v.T
    for tile in range(rows // TILE):
        need = key_rows(causal, tile, rows, keys)
        span = slice(tile * TILE, (tile + 1) * TILE)
        allowed = own_ref[:, span] == seg_ref[:need, :]
        parts = []
        for head in range(LANES // size):
            scores = dot_nt(k[:need], head_lanes(queries[span], head, size))
            if causal:
                scores = scores + bias_at(bias_ref, head, tile, rows, need)
            scores = jnp.where(allowed, scores, MASKED)
            raised = jnp.exp(scores - jnp.max(scores, axis=0, keepdims=True))
            share = 1.0 / jnp.sum(raised, axis=0, keepdims=True)
            weights = low(raised * share)
            p_ref[head, :need, span] = weights
            parts.append(dot_nn(flipped[head * size : (head + 1) * size, :need], weights))
        att_ref[span, :] = low(jnp.concatenate(parts, axis=0).T)


def attend_back(queries, k, v, grads, p_ref, dq_ref, dk_ref, dv_ref, g_ref, size):
    rows, keys = queries.shape[0], k.shape[0]
    causal = g_ref is not None
    factor = size**-0.5
    flipped = k.T
    dk_sum = dv_sum = None
    for tile in reversed(range(rows // TILE)):
        need = key_rows(causal, tile, rows, keys)
        span = slice(tile * TILE, (tile + 1) * TILE)
        parts, all_ds, all_p, all_q, all_da = [], [], [], [], []
        for head in range(LANES // size):
            weights_low = p_ref[head, :need, span]
            weights = weights_low.astype(jnp.float32)
            grad_head = head_lanes(grads[span], head, size)
            grad_p = dot_nt(v[:need], grad_head)
            inner = jnp.sum(weights * grad_p, axis=0, keepdims=True)
            grad_s = low(weights * (grad_p - inner))
            parts.append(dot_nn(flipped[head * size : (head + 1) * size, :need], grad_s))
            all_ds.append(grad_s)
            all_p.append(weights_low)
            all_q.append(head_lanes(queries[span], head, size))
            all_da.append(grad_head)
            if causal:
                for sub in range(TILE // LANES):
                    start = (rows // LANES - 1 - (tile * (TILE // LANES) + sub)) * LANES
                    g_ref[head, start : start + need, :] += grad_s[
                        :, sub * LANES : (sub + 1) * LANES
                    ].astype(jnp.float32)
        dq_ref[span, :] = low((jnp.concatenate(parts, axis=0) * factor).T)
        dk = dot_nn(jnp.concatenate(all_ds, axis=1), jnp.concatenate(all_q, axis=0))
        dv = dot_nn(jnp.concatenate(all_p, axis=1), jnp.concatenate(all_da, axis=0))
        if dk_sum is None:
            dk_sum, dv_sum = dk, dv
        elif need < keys:
            dk_sum = jnp.concatenate([dk_sum[:need] + dk, dk_sum[need:]], axis=0)
            dv_sum = jnp.concatenate([dv_sum[:need] + dv, dv_sum[need:]], axis=0)
        else:
            dk_sum, dv_sum = dk_sum + dk, dv_sum + dv
    dk_ref[...] = low(dk_sum * factor)
    dv_ref[...] = low(dv_sum)


def left_roll(values, steps):
    return pltpu.roll(values, values.shape[1] - steps, 1) if steps else values


def by_bucket(g_ref, rel, table_ref, size):
    count = rel.shape[1] // LANES
    buckets = table_ref.shape[2]
    lane = lax.broadcasted_iota(jnp.int32, (1, buckets), 1)
    for head in range(LANES // size):
        line = None
        for group in range(LANES // 8):
            strip = jnp.concatenate(
                [
                    g_ref[head, (count - 1 - b) * LANES + group * 8 : (count - 1 - b) * LANES + group * 8 + 8, :]
                    for b in range(count)
                ],
                axis=1,
            )
            strip = left_roll(strip, group * 8)
            line = strip if line is None else line + strip
        row = lax.broadcasted_iota(jnp.int32, line.shape, 0)
        for bit in range(3):
            line = jnp.where((row >> bit) & 1 == 1, left_roll(line, 1 << bit), line)
        line = jnp.sum(line, axis=0, keepdims=True)
        found = jnp.zeros((1, buckets), jnp.float32)
        for bucket in range(buckets):
            total = jnp.sum(jnp.where(rel == bucket, line, 0.0), axis=1, keepdims=True)
            found = jnp.where(lane == bucket, total, found)
        table_ref[0, head : head + 1, :] = found


def norm_parts(values):
    scale = lax.rsqrt(jnp.mean(values * values, axis=-1, keepdims=True) + EPSILON)
    return values * scale, scale


def norm_backward(values, gain, grad):
    normed, scale = norm_parts(values)
    scaled = grad * gain
    mean = jnp.mean(scaled * normed, axis=-1, keepdims=True)
    return scale * (scaled - normed * mean), jnp.sum(grad * normed, axis=0, keepdims=True)


def group_lanes(step):
    return pl.ds(pl.multiple_of(step * LANES, LANES), LANES)


def self_project_kernel(prior_ref, own_ref, left_ref, right_ref, n_ref, q_ref, k_ref, v_ref, gain_ref):
    rows, part = q_ref.shape
    more = left_ref.shape[1] - part
    rest = part - more
    gains = right_ref[:, rest : rest + LANES].astype(jnp.float32).T[:8]
    gain_ref[...] = gains
    gain = gains[0:1]
    for at, source in ((0, prior_ref), (rows, own_ref)):
        span = slice(at, at + rows)
        n_ref[span, :] = low(norm_parts(source[...].astype(jnp.float32))[0] * gain)
    normed = n_ref[...]
    q_ref[...] = low(dot_nn(normed[rows:], left_ref[:, :part]))
    k_ref[:, :more] = low(dot_nn(normed, left_ref[:, part:]))
    k_ref[:, more:] = low(dot_nn(normed, right_ref[:, :rest]))
    v_ref[...] = low(dot_nn(normed, right_ref[:, rest + LANES :]))


def self_project(prior, own, left, right, part):
    rows, depth = own.shape
    shape = jax.ShapeDtypeStruct
    vmem = pl.BlockSpec(memory_space=pltpu.VMEM)
    return pl.pallas_call(
        self_project_kernel,
        in_specs=[vmem] * 4,
        out_specs=[vmem] * 5,
        out_shape=[
            shape((2 * rows, depth), jnp.bfloat16),
            shape((rows, part), jnp.bfloat16),
            shape((2 * rows, part), jnp.bfloat16),
            shape((2 * rows, part), jnp.bfloat16),
            shape((8, depth), jnp.float32),
        ],
        name="self_project",
        **params(4 * 10**9, 10 * 10**6),
    )(prior, own, left, right)


def self_forward_kernel(size, q_ref, k_ref, v_ref, seg_ref, row_ref, bias_ref, att_ref, p_ref):
    attend(q_ref[...], k_ref[...], v_ref[...], seg_ref, row_ref, bias_ref, att_ref, p_ref, size)


def self_forward(q, k, v, seg_col, own_row, bias, size):
    rows, part = q.shape
    keys = k.shape[0]
    heads = part // size
    pair = LANES // size
    shape = jax.ShapeDtypeStruct
    tall = lambda count: pl.BlockSpec((count, LANES), lambda i: (0, i))
    return pl.pallas_call(
        functools.partial(self_forward_kernel, size),
        grid=(part // LANES,),
        in_specs=[
            tall(rows),
            tall(keys),
            tall(keys),
            full_block(seg_col.shape),
            full_block(own_row.shape),
            pl.BlockSpec((pair,) + bias.shape[1:], lambda i: (i, 0, 0)),
        ],
        out_specs=[tall(rows), pl.BlockSpec((pair, keys, rows), lambda i: (i, 0, 0))],
        out_shape=[
            shape((rows, part), jnp.bfloat16),
            shape((heads, keys, rows), jnp.bfloat16),
        ],
        name="self_forward",
        **params(12 * 10**9, 20 * 10**6),
    )(q, k, v, seg_col, own_row, bias)


def cross_forward_kernel(
    size, at_q, at_o, x_ref, a_ref, b_ref, gain_ref, w_ref, k_ref, v_ref, seg_ref, row_ref,
    x1_ref, n_ref, q_ref, att_ref, p_ref, out_ref,
):
    step = pl.program_id(0)
    part = q_ref.shape[1]

    @pl.when(step == 0)
    def _():
        x1 = x_ref[...].astype(jnp.float32) + (a_ref[...] + b_ref[...])
        x1_ref[...] = x1
        normed = low(norm_parts(x1)[0] * gain_ref[1:2])
        n_ref[...] = normed
        q_ref[...] = low(dot_nn(normed, w_ref[:, at_q : at_q + part]))

    lanes = group_lanes(step)
    attend(q_ref[:, lanes], k_ref[...], v_ref[...], seg_ref, row_ref, None, att_ref.at[:, lanes], p_ref, size)

    @pl.when(step == pl.num_programs(0) - 1)
    def _():
        out_ref[...] = dot_nt(att_ref[...], w_ref[:, at_o : at_o + part])


def cross_forward(x, a, b, gains, weights, at_q, at_o, k, v, seg_col, own_row, size):
    rows, depth = x.shape
    keys, part = k.shape
    heads = part // size
    pair = LANES // size
    shape = jax.ShapeDtypeStruct
    return pl.pallas_call(
        functools.partial(cross_forward_kernel, size, at_q, at_o),
        grid=(part // LANES,),
        in_specs=[
            full_block(x.shape),
            full_block(a.shape),
            full_block(b.shape),
            full_block(gains.shape),
            full_block(weights.shape),
            pl.BlockSpec((keys, LANES), lambda i: (0, i)),
            pl.BlockSpec((keys, LANES), lambda i: (0, i)),
            full_block(seg_col.shape),
            full_block(own_row.shape),
        ],
        out_specs=[
            full_block((rows, depth)),
            full_block((rows, depth)),
            full_block((rows, part)),
            full_block((rows, part)),
            pl.BlockSpec((pair, keys, rows), lambda i: (i, 0, 0)),
            full_block((rows, depth)),
        ],
        out_shape=[
            shape((rows, depth), jnp.float32),
            shape((rows, depth), jnp.bfloat16),
            shape((rows, part), jnp.bfloat16),
            shape((rows, part), jnp.bfloat16),
            shape((heads, keys, rows), jnp.bfloat16),
            shape((rows, depth), jnp.float32),
        ],
        name="cross_forward",
        **params(12 * 10**9, 20 * 10**6),
    )(x, a, b, gains, weights, k, v, seg_col, own_row)


def feed_forward_kernel(
    x1_ref, a_ref, b_ref, gain_ref, g_ref, up_ref, down_ref,
    x2_ref, n_ref, act_ref, dpre_ref, mixed_ref, dn_ref,
):
    step = pl.program_id(0)

    @pl.when(step == 0)
    def _():
        x2 = x1_ref[...] + (a_ref[...] + b_ref[...])
        x2_ref[...] = x2
        n_ref[...] = low(norm_parts(x2)[0] * gain_ref[2:3])
        mixed_ref[...] = jnp.zeros_like(mixed_ref)
        dn_ref[...] = jnp.zeros_like(dn_ref)

    pre = dot_nn(n_ref[...], up_ref[...])
    square = pre * pre
    bend = jnp.tanh(GELU_ROOT * (pre + GELU_CUBE * (pre * square)))
    half = 0.5 * (1.0 + bend)
    act = low(pre * half)
    slope = half + (0.5 * GELU_ROOT) * pre * (1.0 - bend * bend) * (1.0 + (3 * GELU_CUBE) * square)
    grad_pre = low(slope * dot_nn(g_ref[...], down_ref[...]))
    act_ref[...] = act
    dpre_ref[...] = grad_pre
    mixed_ref[...] += dot_nt(act, down_ref[...])
    dn_ref[...] += dot_nt(grad_pre, up_ref[...])


def feed_forward(x1, a, b, gains, grad, up, down):
    rows, depth = x1.shape
    wide = up.shape[1]
    chunk = 384 if wide % 384 == 0 else wide
    shape = jax.ShapeDtypeStruct
    tall = pl.BlockSpec((depth, chunk), lambda i: (0, i))
    slab = pl.BlockSpec((rows, chunk), lambda i: (0, i))
    whole = full_block((rows, depth))
    return pl.pallas_call(
        feed_forward_kernel,
        grid=(wide // chunk,),
        in_specs=[whole, whole, whole, full_block(gains.shape), whole, tall, tall],
        out_specs=[whole, whole, slab, slab, whole, whole],
        out_shape=[
            shape((rows, depth), jnp.float32),
            shape((rows, depth), jnp.bfloat16),
            shape((rows, wide), jnp.bfloat16),
            shape((rows, wide), jnp.bfloat16),
            shape((rows, depth), jnp.float32),
            shape((rows, depth), jnp.float32),
        ],
        name="feed_forward",
        **params(8 * 10**9, 20 * 10**6),
    )(x1, a, b, gains, grad, up, down)


def attention_back_kernel(
    size, causal, gain_row, pieces, at_q, *refs,
):
    if causal:
        (x_ref, a_ref, b_ref, gain_ref, g_ref, q_ref, k_ref, v_ref, p_ref, rel_ref, *rest) = refs
    else:
        (x_ref, a_ref, b_ref, gain_ref, g_ref, q_ref, k_ref, v_ref, p_ref, *rest) = refs
    count = len({which for which, _, _ in pieces})
    weights, rest = rest[:count], rest[count:]
    if causal:
        sum_ref, low_ref, dgain_ref, dq_ref, dk_ref, dv_ref, table_ref, da_ref, diag_ref = rest
    else:
        sum_ref, low_ref, dgain_ref, dq_ref, dk_ref, dv_ref, dn_ref, da_ref = rest
    step = pl.program_id(0)

    @pl.when(step == 0)
    def _():
        add, dgain = norm_backward(x_ref[...], gain_ref[gain_row : gain_row + 1], a_ref[...] + b_ref[...])
        total = g_ref[...].astype(jnp.float32) + add
        sum_ref[...] = total
        total = low(total)
        low_ref[...] = total
        dgain_ref[...] = jnp.broadcast_to(dgain, dgain_ref.shape)
        at = 0
        for which, start, stop in pieces:
            da_ref[:, at : at + stop - start] = low(dot_nn(total, weights[which][:, start:stop]))
            at += stop - start

    lanes = group_lanes(step)
    if causal:
        diag_ref[...] = jnp.zeros_like(diag_ref)
    attend_back(
        q_ref[...], k_ref[...], v_ref[...], da_ref[:, lanes], p_ref,
        dq_ref if causal else dq_ref.at[:, lanes], dk_ref, dv_ref, diag_ref if causal else None, size,
    )
    if causal:
        by_bucket(diag_ref, rel_ref[...], table_ref, size)
    else:

        @pl.when(step == pl.num_programs(0) - 1)
        def _():
            part = dq_ref.shape[1]
            dn_ref[...] = dot_nt(dq_ref[...], weights[0][:, at_q : at_q + part])


def attention_back(x, a, b, gains, gain_row, grad, q, k, v, p, weights, pieces, at_q, rel_row, buckets, size):
    rows, depth = x.shape
    keys, part = k.shape
    causal = rel_row is not None
    pair = LANES // size
    groups = part // LANES
    shape = jax.ShapeDtypeStruct
    whole = full_block((rows, depth))
    tall = lambda count: pl.BlockSpec((count, LANES), lambda i: (0, i))
    in_specs = [
        whole,
        whole,
        whole,
        full_block(gains.shape),
        whole,
        tall(rows),
        tall(keys),
        tall(keys),
        pl.BlockSpec((pair, keys, rows), lambda i: (i, 0, 0)),
    ]
    args = [x, a, b, gains, grad, q, k, v, p]
    if causal:
        in_specs.append(full_block(rel_row.shape))
        args.append(rel_row)
    in_specs += [full_block(item.shape) for item in weights]
    args += list(weights)
    out_specs = [
        whole,
        whole,
        full_block((8, depth)),
        tall(rows) if causal else full_block((rows, part)),
        tall(keys),
        tall(keys),
    ]
    out_shape = [
        shape((rows, depth), jnp.float32),
        shape((rows, depth), jnp.bfloat16),
        shape((8, depth), jnp.float32),
        shape((rows, part), jnp.bfloat16),
        shape((keys, part), jnp.bfloat16),
        shape((keys, part), jnp.bfloat16),
    ]
    scratch = [pltpu.VMEM((rows, part), jnp.bfloat16)]
    if causal:
        out_specs.append(pl.BlockSpec((1, pair, buckets), lambda i: (i, 0, 0)))
        out_shape.append(shape((groups, pair, buckets), jnp.float32))
        scratch.append(pltpu.VMEM((pair, rel_row.shape[1] + LANES, LANES), jnp.float32))
    else:
        out_specs.append(whole)
        out_shape.append(shape((rows, depth), jnp.float32))
    return pl.pallas_call(
        functools.partial(attention_back_kernel, size, causal, gain_row, pieces, at_q),
        grid=(groups,),
        in_specs=in_specs,
        out_specs=out_specs,
        out_shape=out_shape,
        scratch_shapes=scratch,
        name="self_backward" if causal else "cross_backward",
        **params(12 * 10**9, 20 * 10**6),
    )(*args)


def split_grad_kernel(plan, place_ref, *refs):
    count = 1 + max(max(entry[1], entry[2]) for entry in plan)
    halves = 1 + max(entry[0] for entry in plan)
    inputs, outputs, (sum_ref, *flips) = refs[:count], refs[count : count + 2 * halves], refs[count + 2 * halves :]
    flipped = dict(zip(sorted({entry[1] for entry in plan}), flips))

    @pl.when(pl.program_id(0) == 0)
    def _():
        for left in flipped:
            flipped[left][...] = inputs[left][...].T

    for bit, left, right, first_row, start in plan:
        keep_ref, send_ref = outputs[2 * bit], outputs[2 * bit + 1]
        blocks, block_rows = keep_ref.shape[0], keep_ref.shape[1]
        mine = (place_ref[0] >> bit) & 1
        wide = inputs[right].shape[1]
        span = slice(start, start + wide)
        sum_ref[:, :wide] = low(dot_nn(flipped[left][:, first_row:], inputs[right][...]))
        for block in range(blocks):
            base = (block >> bit << (bit + 1)) | (block & ((1 << bit) - 1))
            kept = (base + (mine << bit)) * block_rows
            sent = (base + ((1 - mine) << bit)) * block_rows
            keep_ref[block, :, span] = sum_ref[pl.ds(pl.multiple_of(kept, 16), block_rows), :wide]
            send_ref[block, :, span] = sum_ref[pl.ds(pl.multiple_of(sent, 16), block_rows), :wide]


def split_grads(place, bits, inputs, plan, chunk=None):
    depth = inputs[plan[0][1]].shape[1]
    blocks = 1 << bits
    block_rows = depth // blocks
    wide = [sum(inputs[right].shape[1] for half, _, right, _, _ in plan if half == bit) for bit in (0, 1)]
    if block_rows % 16:
        found = []
        for bit in (0, 1):
            full = jnp.concatenate(
                [low(dot_tn(inputs[left][row:], inputs[right])) for half, left, right, row, _ in plan if half == bit],
                axis=1,
            ).reshape(1 << (bits - 1 - bit), 2, 1 << bit, block_rows, wide[bit])
            mine = (place >> bit) & 1
            found.append(
                tuple(
                    lax.dynamic_index_in_dim(full, index, 1, keepdims=False).reshape(-1, block_rows, wide[bit])
                    for index in (mine, 1 - mine)
                )
            )
        return found
    lefts = {left for _, left, _, _, _ in plan}
    out_specs, out_shape = [], []
    for bit in (0, 1):
        for _ in range(2):
            out_shape.append(jax.ShapeDtypeStruct((blocks // 2, block_rows, wide[bit]), jnp.bfloat16))
            out_specs.append(
                pl.BlockSpec((blocks // 2, block_rows, chunk or wide[bit]), lambda i: (0, 0, i if chunk else 0))
            )
    in_specs = [
        full_block(item.shape)
        if index in lefts or not chunk
        else pl.BlockSpec((item.shape[0], chunk), lambda i: (0, i))
        for index, item in enumerate(inputs)
    ]
    most = chunk or max(inputs[right].shape[1] for _, _, right, _, _ in plan)
    found = pl.pallas_call(
        functools.partial(split_grad_kernel, plan),
        grid=(wide[0] // chunk if chunk else 1,),
        in_specs=[pl.BlockSpec(memory_space=pltpu.SMEM)] + in_specs,
        out_specs=out_specs,
        out_shape=out_shape,
        scratch_shapes=[pltpu.VMEM((depth, most), jnp.bfloat16)]
        + [pltpu.VMEM(inputs[left].shape[::-1], jnp.bfloat16) for left in sorted(lefts)],
        name="split_grads",
        **params(4 * 10**9, 10 * 10**6),
    )(place.reshape(1), *inputs)
    return (found[0], found[1]), (found[2], found[3])


def input_grad_kernel(pieces, *refs):
    count = 1 + max(entry[0] for entry in pieces)
    tokens, refs = refs[:count], refs[count:]
    weights, out_ref = refs[:-1], refs[-1]
    total = None
    for which, start, stop, weight, at in pieces:
        term = dot_nt(tokens[which][:, start:stop], weights[weight][:, at : at + stop - start])
        total = term if total is None else total + term
    out_ref[...] = total


def input_grad(tokens, weights, pieces):
    rows = tokens[0].shape[0]
    depth = weights[0].shape[0]
    vmem = pl.BlockSpec(memory_space=pltpu.VMEM)
    return pl.pallas_call(
        functools.partial(input_grad_kernel, pieces),
        in_specs=[vmem] * (len(tokens) + len(weights)),
        out_specs=vmem,
        out_shape=jax.ShapeDtypeStruct((rows, depth), jnp.float32),
        name="input_grad",
        **params(1 * 10**9, 6 * 10**6),
    )(*tokens, *weights)


SEQ = ("far", "near")


def axis_bits(axis):
    return lax.axis_size(axis).bit_length() - 1


def partner_swap(value, axis, bit):
    count = lax.axis_size(axis)
    return lax.ppermute(value, axis, [(i, i ^ (1 << bit)) for i in range(count)])


def shifted(value, axis, steps):
    count = lax.axis_size(axis)
    leading, last = (max(0, -steps), min(count, count - steps))
    return lax.ppermute(value, axis, [(source, source + steps) for source in range(leading, last)])


def my_bit(axis, bit):
    return (lax.axis_index(axis) >> bit) & 1


def head_swap(value):
    return lax.ppermute(value, "heads", [(0, 1), (1, 0)])


def pin(value, *after):
    return lax.optimization_barrier((value, after))[0]


def joined(value, other, axis, bit, place):
    mine = my_bit(axis, bit) == 0
    return jnp.stack([jnp.where(mine, value, other), jnp.where(mine, other, value)], axis=place)


def gather_far(shard, axis):
    value = shard
    for place, bit in enumerate(range(axis_bits(axis) - 1, 1, -1)):
        value = joined(value, partner_swap(value, axis, bit), axis, bit, place)
    return value


def gather_near_first(value, axis, cut):
    place = axis_bits(axis) - 2
    left, right = value[..., :cut], value[..., cut:]
    return (
        joined(left, partner_swap(left, axis, 1), axis, 1, place),
        joined(right, partner_swap(right, axis, 0), axis, 0, place),
    )


def gather_near_last(halves, axis):
    left, right = halves
    place = axis_bits(axis) - 2
    left = joined(left, partner_swap(left, axis, 0), axis, 0, place + 1)
    right = joined(right, partner_swap(right, axis, 1), axis, 1, place)
    return tuple(item.reshape(-1, item.shape[-1]) for item in (left, right))


def keep_and_send(terms, axis, bit, place):
    mine = my_bit(axis, bit)
    keep, send = (
        sum(lax.dynamic_index_in_dim(term, index, place, keepdims=False).astype(jnp.float32) for term in terms)
        for index in (mine, 1 - mine)
    )
    return keep, low(send)


def near_last_parts(halves, axis):
    bits = axis_bits(axis)
    found = []
    for bit, terms in enumerate(halves):
        terms = [term.reshape((2,) * (bits - 1) + term.shape[-2:]) for term in terms]
        found.append(keep_and_send(terms, axis, 1 - bit, bits - 2))
    return found


def far_parts(terms, axis, bit):
    return keep_and_send(terms, axis, bit, terms[0].ndim - 3)


def send_far(parts, axis, bit):
    return parts[0], partner_swap(parts[1], axis, bit)


def columns(terms):
    return [jnp.concatenate(pieces, axis=-1) for pieces in zip(*terms)]


def sum_all(value, axis):
    for bit in range(axis_bits(axis)):
        value = value + partner_swap(value, axis, bit)
    return value


def matmul(spec, left, right):
    return jnp.einsum(spec, left, right, preferred_element_type=jnp.float32)


def block_before(value):
    rows = value.shape[-2] // 2
    core = lax.axis_index("heads")
    half = shifted(lax.dynamic_slice_in_dim(value, core * rows, rows, value.ndim - 2), SEQ, 1)
    other = head_swap(half)
    first = jnp.where(core == 0, half, other)
    second = jnp.where(core == 0, other, half)
    return first, second


def to_owner(part):
    rows = part.shape[0] // 2
    core = lax.axis_index("heads")
    mine = lax.dynamic_slice_in_dim(part, core * rows, rows)
    other = lax.dynamic_slice_in_dim(part, (1 - core) * rows, rows)
    return low(mine + head_swap(other))


def add_half(part, half):
    rows = half.shape[0]
    core = lax.axis_index("heads")
    half = half.astype(jnp.float32)
    blank = jnp.zeros_like(half)
    return part + jnp.concatenate([jnp.where(core == 0, half, blank), jnp.where(core == 0, blank, half)])


def per_device(
    hidden_in,
    memory,
    out_grad,
    norm_self,
    self_q,
    self_k,
    self_v,
    self_o,
    norm_cross,
    cross_q,
    cross_k,
    cross_v,
    cross_o,
    norm_ff,
    ff_in,
    ff_out,
    bias_table,
    seg_ids,
    mem_seg,
    rel_bucket,
):
    rows = hidden_in.shape[0]
    mem_rows = memory.shape[0]
    heads = bias_table.shape[1]
    buckets = bias_table.shape[0]
    part = self_q.shape[1]
    wide = ff_in.shape[1]
    size = part // heads
    bits = axis_bits(SEQ)
    position = lax.axis_index(SEQ)

    gains = jnp.pad(jnp.stack([norm_self, norm_cross, norm_ff], axis=1), ((0, 0), (0, LANES - 3)))
    first = gather_far(low(jnp.concatenate([self_q, self_k, gains, self_v], axis=1)), SEQ)
    before = block_before(jnp.stack([hidden_in, memory]))
    second = low(jnp.concatenate([cross_k, cross_v, self_o.T, cross_q, cross_o.T], axis=1))
    second = gather_far(pin(second, first), SEQ)
    cut_one = (2 * part + LANES + part) // 256 * 128
    first = gather_near_first(first, SEQ, cut_one)
    third = gather_far(pin(low(jnp.concatenate([ff_in, ff_out.T], axis=1)), second), SEQ)
    cut_two = 5 * part // 256 * 128
    second = gather_near_first(pin(second, first), SEQ, cut_two)
    first = gather_near_last(first, SEQ)

    def pair_of_blocks(ids, count):
        own = lax.dynamic_slice_in_dim(ids, position * count, count)
        prior = lax.dynamic_slice_in_dim(ids, jnp.maximum(position - 1, 0) * count, count)
        return jnp.concatenate([jnp.where(position > 0, prior, -2), own])

    seg_pair = pair_of_blocks(seg_ids, rows)
    mem_pair = pair_of_blocks(mem_seg, mem_rows)
    own_row = seg_pair[rows:].reshape(1, rows)
    seg_col = seg_pair.reshape(-1, 1)
    mem_col = mem_pair.reshape(-1, 1)
    rel_row = rel_bucket.reshape(1, -1)
    bias = bias_tiles(rel_row, bias_table)
    prior = jnp.concatenate([before[0][0], before[1][0]])
    mem_both = jnp.concatenate([before[0][1], before[1][1], memory])

    normed_pair, query_one, key_one, value_one, gain_rows = self_project(
        prior, hidden_in, first[0], first[1], part
    )
    query_one = pin(query_one, second)
    second = gather_near_last(second, SEQ)
    attend_one, weights_one = self_forward(
        query_one, key_one, value_one, seg_col, own_row, bias, size
    )
    third = gather_near_first(pin(third, second), SEQ, wide)
    more = cut_two - 2 * part
    rest = part - more
    left_two, right_two = second
    out_pieces = ((0, 2 * part, cut_two), (1, 0, rest))
    part_one = input_grad(
        [attend_one], [left_two, right_two], ((0, 0, more, 0, 2 * part), (0, more, part, 1, 0))
    )
    other_one = head_swap(part_one)
    mem_key, mem_value = (
        low(matmul("md,dw->mw", mem_both, left_two[:, at : at + part])) for at in (0, part)
    )

    mem_key = pin(mem_key, third)
    third = gather_near_last(third, SEQ)
    stream_one, normed_two, query_two, attend_two, weights_two, part_two = cross_forward(
        hidden_in, part_one, other_one, gain_rows, right_two, rest, rest + part, mem_key, mem_value,
        mem_col, own_row, size,
    )
    other_two = head_swap(part_two)

    stream_two, normed_three, active, grad_pre, part_three, back_three = feed_forward(
        stream_one, part_two, other_two, gain_rows, out_grad, third[0], third[1]
    )
    back_other = head_swap(back_three)
    other_three = head_swap(part_three)
    ff_split = split_grads(
        position, bits, (normed_three, grad_pre, out_grad, active),
        ((0, 0, 1, 0, 0), (1, 2, 3, 0, 0)), 384 if wide % 384 == 0 else None,
    )
    ff_terms = [(keep, partner_swap(send, SEQ, bit)) for bit, (keep, send) in enumerate(ff_split)]
    back_three, back_other = pin((back_three, back_other), ff_split)

    grad_two, low_two, gain_ff, grad_query_two, grad_mem_key, grad_mem_value, back_two = attention_back(
        stream_two, back_three, back_other, gain_rows, 2, out_grad, query_two, mem_key, mem_value,
        weights_two, [right_two], ((0, rest + part, rest + 2 * part),), rest, None, buckets, size,
    )
    other_back = head_swap(back_two)
    cross_split = split_grads(
        position, bits, (normed_two, grad_query_two, mem_both, grad_mem_key, grad_mem_value, low_two, attend_two),
        ((0, 0, 1, 0, 0), (0, 2, 3, 0, part), (1, 2, 4, 0, 0), (1, 5, 6, 0, part)),
    )
    cross_terms = [(keep, partner_swap(send, SEQ, bit)) for bit, (keep, send) in enumerate(cross_split)]
    mem_pieces = ((0, 0, part, 0, 0), (1, 0, part, 0, part))
    mem_back = input_grad([grad_mem_key[:mem_rows], grad_mem_value[:mem_rows]], [left_two], mem_pieces)
    mem_back = to_owner(mem_back)
    mem_came = shifted(mem_back, SEQ, -1)
    ff_terms = [(keep, pin(got, mem_back)) for keep, got in ff_terms]
    ff_parts = near_last_parts(ff_terms, SEQ)
    ff_terms = [(keep, partner_swap(send, SEQ, 1 - bit)) for bit, (keep, send) in enumerate(ff_parts)]
    back_two, other_back = pin((back_two, other_back), cross_split, ff_parts, mem_back)

    grad_one, low_one, gain_cross, grad_query_one, grad_key_one, grad_value_one, table_part = attention_back(
        stream_one, back_two, other_back, gain_rows, 1, grad_two, query_one, key_one, value_one,
        weights_one, [left_two, right_two], out_pieces, None, rel_row, buckets, size,
    )
    self_split = split_grads(
        position, bits, (normed_pair, grad_query_one, grad_key_one, grad_value_one, low_one, attend_one),
        ((0, 0, 1, rows, 0), (0, 0, 2, 0, part), (1, 0, 3, 0, 0), (1, 4, 5, 0, part)),
    )
    ff_terms = [(keep, pin(got, grad_query_one)) for keep, got in ff_terms]
    cross_terms = [(keep, pin(got, grad_query_one)) for keep, got in cross_terms]
    ff_parts = far_parts(columns(ff_terms), SEQ, 2)
    ff_terms = send_far(ff_parts, SEQ, 2)
    cross_parts = near_last_parts(cross_terms, SEQ)
    cross_terms = [(keep, partner_swap(send, SEQ, 1 - bit)) for bit, (keep, send) in enumerate(cross_parts)]
    self_terms = [(keep, partner_swap(send, SEQ, bit)) for bit, (keep, send) in enumerate(self_split)]

    more_one = cut_one - part
    rest_one = part - more_one
    key_pieces = ((0, 0, more_one, 0, part), (0, more_one, part, 1, 0), (1, 0, part, 1, rest_one + LANES))
    own_pieces = key_pieces + ((2, 0, part, 0, 0),)
    grad_key_one, grad_value_one = pin((grad_key_one, grad_value_one), self_split)
    self_back = to_owner(input_grad([grad_key_one[:rows], grad_value_one[:rows]], list(first), key_pieces))
    self_came = shifted(self_back, SEQ, -1)
    self_part = input_grad(
        [grad_key_one[rows:], grad_value_one[rows:], grad_query_one], list(first), own_pieces
    )
    mem_part = input_grad([grad_mem_key[mem_rows:], grad_mem_value[mem_rows:]], [left_two], mem_pieces)
    mem_part = add_half(mem_part, pin(mem_came, self_back))
    grad_memory = mem_part + head_swap(mem_part)
    self_part = add_half(self_part, self_came)
    grad_normed = self_part + head_swap(self_part)
    add, gain_self = norm_backward(hidden_in.astype(jnp.float32), gain_rows[0:1], grad_normed)
    grad_hidden = grad_one + add

    for bit in range(3, bits):
        ff_terms = send_far(far_parts(ff_terms, SEQ, bit), SEQ, bit)
    cross_terms = columns(cross_terms)
    for bit in range(2, bits):
        cross_terms = send_far(far_parts(cross_terms, SEQ, bit), SEQ, bit)
    self_parts = near_last_parts(self_terms, SEQ)
    self_terms = [(keep, partner_swap(send, SEQ, 1 - bit)) for bit, (keep, send) in enumerate(self_parts)]
    self_terms = columns(self_terms)
    for bit in range(2, bits):
        self_terms = send_far(far_parts(self_terms, SEQ, bit), SEQ, bit)
    gain_grads = jnp.stack([gain_self[0], gain_cross[0], gain_ff[0]], axis=1)
    gain_terms = [jnp.pad(gain_grads, ((0, 0), (0, LANES - 3))).reshape((2,) * bits + (-1, LANES))]
    for bit in range(bits):
        gain_terms = send_far(far_parts(gain_terms, SEQ, bit), SEQ, bit)
    grad_table = sum_all(table_part.reshape(heads, -1).T, SEQ)
    ff_summed, cross_summed, self_summed, gain_summed = (
        keep + got.astype(jnp.float32) for keep, got in (ff_terms, cross_terms, self_terms, gain_terms)
    )
    return (
        low(stream_two + (part_three + other_three)),
        grad_hidden,
        grad_memory,
        gain_summed[:, 0],
        self_summed[:, :part],
        self_summed[:, part : 2 * part],
        self_summed[:, 2 * part : 3 * part],
        self_summed[:, 3 * part :].T,
        gain_summed[:, 1],
        cross_summed[:, :part],
        cross_summed[:, part : 2 * part],
        cross_summed[:, 2 * part : 3 * part],
        cross_summed[:, 3 * part :].T,
        gain_summed[:, 2],
        ff_summed[:, :wide],
        ff_summed[:, wide:].T,
        grad_table,
    )


def solution(mesh):
    count = mesh.shape["seq"]
    near = min(4, count)
    grid = Mesh(mesh.devices.reshape(count // near, near, -1), SEQ + ("heads",))
    in_specs = (
        P(SEQ, None),
        P(SEQ, None),
        P(SEQ, None),
        P(SEQ),
        P(SEQ, "heads"),
        P(SEQ, "heads"),
        P(SEQ, "heads"),
        P("heads", SEQ),
        P(SEQ),
        P(SEQ, "heads"),
        P(SEQ, "heads"),
        P(SEQ, "heads"),
        P("heads", SEQ),
        P(SEQ),
        P(SEQ, "heads"),
        P("heads", SEQ),
        P(None, "heads"),
        P(),
        P(),
        P(),
    )
    out_specs = (
        P(SEQ, None),
        P(SEQ, None),
        P(SEQ, None),
        P(SEQ),
        P(SEQ, "heads"),
        P(SEQ, "heads"),
        P(SEQ, "heads"),
        P("heads", SEQ),
        P(SEQ),
        P(SEQ, "heads"),
        P(SEQ, "heads"),
        P(SEQ, "heads"),
        P("heads", SEQ),
        P(SEQ),
        P(SEQ, "heads"),
        P("heads", SEQ),
        P(None, "heads"),
    )
    return jax.shard_map(
        per_device, mesh=grid, in_specs=in_specs, out_specs=out_specs, check_vma=False
    )
```
